32 devices in a mesh: ctx: 16 (over z, x, core), head: 2 (over y).
Axes of the slice: x: 2, y: 2, z: 4, core: 2. Of those that a mesh axis runs over, the one named last changes fastest.
Arguments:
- vid_query: bfloat16 [8, 4096, 128], P('head', 'ctx')
- vid_key: bfloat16 [8, 4096, 128], P('head', 'ctx')
- vid_value: bfloat16 [8, 4096, 128], P('head', 'ctx'), may hold values from -6 to 6
- vid_out: bfloat16 [8, 4096, 128], P('head', 'ctx'), may hold values from -6 to 6
- vid_grad: bfloat16 [8, 4096, 128], P('head', 'ctx'), may hold values from -96 to 96
- vid_lse: float32 [8, 4096], P('head', 'ctx'), as said below
- vid_mask: int32 [8, 4096, 128], P('head', 'ctx'), may hold values from 0 to 255
- aud_query: bfloat16 [8, 1024, 128], P('head', 'ctx')
- aud_key: bfloat16 [8, 1024, 128], P('head', 'ctx')
- aud_value: bfloat16 [8, 1024, 128], P('head', 'ctx'), may hold values from -6 to 6
- aud_out: bfloat16 [8, 1024, 128], P('head', 'ctx'), may hold values from -6 to 6
- aud_grad: bfloat16 [8, 1024, 128], P('head', 'ctx'), may hold values from -384 to 384
- aud_lse: float32 [8, 1024], P('head', 'ctx'), as said below
- aud_mask: int32 [8, 1024, 512], P('head', None, 'ctx'), may hold values from 0 to 255
- gain_vq: float32 [8, 128], P('head'), may hold values from 0.5 to 1.5
- gain_ak: float32 [8, 128], P('head'), may hold values from 0.5 to 1.5
- gain_aq: float32 [8, 128], P('head'), may hold values from 0.5 to 1.5
- gain_vk: float32 [8, 128], P('head'), may hold values from 0.5 to 1.5
Outputs:
- grad_vid_query: bfloat16 [8, 4096, 128], P('head', 'ctx')
- grad_vid_key: bfloat16 [8, 4096, 128], P('head', 'ctx')
- grad_vid_value: bfloat16 [8, 4096, 128], P('head', 'ctx')
- grad_aud_query: bfloat16 [8, 1024, 128], P('head', 'ctx')
- grad_aud_key: bfloat16 [8, 1024, 128], P('head', 'ctx')
- grad_aud_value: bfloat16 [8, 1024, 128], P('head', 'ctx')
The draws below stay inside these ranges and needn't reach their ends.
Inputs may be any that keep to these rules, and one draw needn't show every extreme that they name: `vid_lse`: every entry lies between ln(1024) and ln(1024) + 1.5. `aud_lse`: every entry lies between ln(4096) and ln(4096) + 1.5.
All inputs are finite; a program needn't handle non-finite values.
Results may differ from the reference program's by a relative error of at most 0.011.
Values may be sent and summed in bfloat16 or wider, within the bound.
A program may use at most 128 MiB of HBM per device.

```python
import math
import jax
import jax.numpy as jnp
from jax import lax

DH = 128
HEADS = 8
VIDEO = 4096
AUDIO = 1024


def token_field(seed_key, row_count, head_rise):
    base_key, row_key, column_key = jax.random.split(seed_key, 3)
    field_shape = (HEADS, row_count, DH)
    normal_values = jax.random.normal(base_key, field_shape, jnp.float32)
    base_values = normal_values
    row_scale = jnp.exp(jax.random.uniform(row_key, (1, row_count, 1), jnp.float32, math.log(0.3), math.log(3.0)))
    column_scale = jnp.exp(jax.random.uniform(column_key, (HEADS, 1, DH), jnp.float32, math.log(0.5), math.log(2.0)))
    head_scale = head_rise ** (jnp.arange(HEADS, dtype=jnp.float32) / max(HEADS - 1, 1))
    return (base_values * row_scale * column_scale * head_scale[:, None, None]).astype(jnp.bfloat16)


def draw_vid_query(key, part):
    key = jax.random.fold_in(key, 11)
    return token_field(key, VIDEO, 1.5)


def draw_vid_key(key, part):
    key = jax.random.fold_in(key, 12)
    return token_field(key, VIDEO, 1.5)


def draw_aud_query(key, part):
    key = jax.random.fold_in(key, 13)
    return token_field(key, AUDIO, 1.5)


def draw_aud_key(key, part):
    key = jax.random.fold_in(key, 14)
    return token_field(key, AUDIO, 1.5)


def draw_vid_lse(key, part):
    key = jax.random.fold_in(key, 21)
    offsets = jax.random.uniform(key, (HEADS, VIDEO), jnp.float32, 0.2, 1.0)
    return math.log(AUDIO) + offsets


def draw_aud_lse(key, part):
    key = jax.random.fold_in(key, 22)
    offsets = jax.random.uniform(key, (HEADS, AUDIO), jnp.float32, 0.2, 1.0)
    return math.log(VIDEO) + offsets


def place_ends(entries, key, smallest, top_value):
    place = [jax.random.randint(jax.random.fold_in(key, axis), (), 0, length) for axis, length in enumerate(entries.shape)]
    widest = entries.shape.index(max(entries.shape))
    neighbour = place[:widest] + [(place[widest] + 1) % entries.shape[widest]] + place[widest + 1:]
    return entries.at[tuple(place)].set(smallest).at[tuple(neighbour)].set(top_value)


def levels(stream_key, dims, cuts, low, largest):
    factor_of, own = 1.0, jax.random.fold_in(stream_key, 6)
    for dim, blocks in cuts:
        heights = jnp.exp(jax.random.uniform(jax.random.fold_in(own, dim), (blocks,), jnp.float32, low / len(cuts), largest / len(cuts)))
        factor_of = factor_of * jnp.repeat(heights, dims[dim] // blocks).reshape([-1 if axis == dim else 1 for axis in range(len(dims))])
    return factor_of


def centred(own_key, shape, spread, bound, cuts=(), kind=jnp.bfloat16):
    drawn = spread * jax.random.normal(own_key, shape, jnp.float32)
    if cuts:
        drawn = drawn * levels(own_key, shape, cuts, -0.22, 0.18)
    return jnp.clip(drawn, -bound, bound).astype(kind)


def setup_inputs(seed: int = 0) -> dict:
    keys = jax.random.split(jax.random.key(seed), 19)
    return {
        "vid_query": draw_vid_query(jax.random.fold_in(keys[18], 71), 0),
        "vid_key": draw_vid_key(jax.random.fold_in(keys[18], 71), 0),
        "vid_value": centred(keys[2], (HEADS, VIDEO, DH), 1.0, 6.0, ((0, 2), (1, 16))),
        "vid_out": centred(keys[3], (HEADS, VIDEO, DH), 1.0, 6.0, ((0, 2), (1, 16))),
        "vid_grad": centred(keys[4], (HEADS, VIDEO, DH), 16.0, 96.0, ((0, 2), (1, 16))),
        "vid_lse": draw_vid_lse(jax.random.fold_in(keys[18], 71), 0),
        "vid_mask": place_ends(jax.random.randint(keys[6], (HEADS, VIDEO, AUDIO // 8), 0, 256), jax.random.fold_in(keys[6], 1), 0, 255).astype(jnp.int32),
        "aud_query": draw_aud_query(jax.random.fold_in(keys[18], 71), 0),
        "aud_key": draw_aud_key(jax.random.fold_in(keys[18], 71), 0),
        "aud_value": centred(keys[9], (HEADS, AUDIO, DH), 1.0, 6.0, ((0, 2), (1, 16))),
        "aud_out": centred(keys[10], (HEADS, AUDIO, DH), 1.0, 6.0, ((0, 2), (1, 16))),
        "aud_grad": centred(keys[11], (HEADS, AUDIO, DH), 64.0, 384.0, ((0, 2), (1, 16))),
        "aud_lse": draw_aud_lse(jax.random.fold_in(keys[18], 71), 0),
        "aud_mask": place_ends(jax.random.randint(keys[13], (HEADS, AUDIO, VIDEO // 8), 0, 256), jax.random.fold_in(keys[13], 1), 0, 255).astype(jnp.int32),
        "gain_vq": jnp.clip(1.0 + 0.1 * jax.random.normal(keys[14], (HEADS, DH), jnp.float32), 0.5, 1.5),
        "gain_ak": jnp.clip(1.0 + 0.1 * jax.random.normal(keys[15], (HEADS, DH), jnp.float32), 0.5, 1.5),
        "gain_aq": jnp.clip(1.0 + 0.1 * jax.random.normal(keys[16], (HEADS, DH), jnp.float32), 0.5, 1.5),
        "gain_vk": jnp.clip(1.0 + 0.1 * jax.random.normal(keys[17], (HEADS, DH), jnp.float32), 0.5, 1.5),
    }


EPS = 1e-06

def unpack_bits(word_rows):
    shifts = jnp.arange(8, dtype=jnp.int32)
    bit_values = jnp.bitwise_and(jnp.right_shift(word_rows[..., None], shifts), 1)
    return bit_values.reshape(word_rows.shape[:-1] + (word_rows.shape[-1] * 8,)).astype(jnp.float32)

def row_scales(tokens):
    values = tokens.astype(jnp.float32)
    return lax.rsqrt(lax.optimization_barrier(jnp.mean(values * values, axis=(0, 2))) + EPS)

def normalize(tokens, scales, gain_rows):
    return (tokens.astype(jnp.float32) * scales[None, :, None] * gain_rows[:, None, :]).astype(jnp.bfloat16)

def norm_backward(tokens, scales, gain_rows, upstream):
    weighted = upstream * gain_rows[:, None, :]
    unit_rows = tokens.astype(jnp.float32) * scales[None, :, None]
    mean_term = lax.optimization_barrier(jnp.mean(weighted * unit_rows, axis=(0, 2)))
    return (scales[None, :, None] * (weighted - unit_rows * mean_term[None, :, None])).astype(jnp.bfloat16)

def one_direction(queries, key_rows, value_rows, outputs, upstream, lse_rows, word_rows):
    query_count, head_dim = queries.shape
    score_scale = head_dim ** (-0.5)
    block_rows = math.gcd(query_count, 512)
    block_count = query_count // block_rows
    stacked = (queries.reshape(block_count, block_rows, head_dim), upstream.reshape(block_count, block_rows, head_dim), outputs.reshape(block_count, block_rows, head_dim), lse_rows.reshape(block_count, block_rows), word_rows.reshape(block_count, block_rows, word_rows.shape[-1]))

    def sweep_block(running, pieces):
        key_grad, value_grad = running
        query_block, grad_block, out_block, lse_block, word_block = pieces
        scores = jnp.dot(query_block, key_rows.T, preferred_element_type=jnp.float32) * score_scale
        attention = jnp.exp(scores - lse_block[:, None])
        kept_mask = unpack_bits(word_block)
        dropped = (2.0 * kept_mask * attention).astype(jnp.bfloat16)
        value_grad = value_grad + jnp.dot(dropped.T, grad_block, preferred_element_type=jnp.float32)
        delta_rows = lax.optimization_barrier(jnp.sum(grad_block.astype(jnp.float32) * out_block.astype(jnp.float32), axis=1))
        prob_grad = 2.0 * kept_mask * jnp.dot(grad_block, value_rows.T, preferred_element_type=jnp.float32)
        score_grad = (attention * (prob_grad - delta_rows[:, None])).astype(jnp.bfloat16)
        query_grad = score_scale * jnp.dot(score_grad, key_rows, preferred_element_type=jnp.float32)
        key_grad = key_grad + score_scale * jnp.dot(score_grad.T, query_block, preferred_element_type=jnp.float32)
        return ((key_grad, value_grad), query_grad)
    empty_rows = jnp.zeros(key_rows.shape, jnp.float32)
    (key_grad, value_grad), query_grad = lax.scan(sweep_block, (empty_rows, empty_rows), stacked)
    return (query_grad.reshape(query_count, head_dim), key_grad, value_grad)

def reference(vid_query, vid_key, vid_value, vid_out, vid_grad, vid_lse, vid_mask, aud_query, aud_key, aud_value, aud_out, aud_grad, aud_lse, aud_mask, gain_vq, gain_ak, gain_aq, gain_vk):
    scale_vq = row_scales(vid_query)
    scale_ak = row_scales(aud_key)
    scale_aq = row_scales(aud_query)
    scale_vk = row_scales(vid_key)
    normed_vq = normalize(vid_query, scale_vq, gain_vq)
    normed_ak = normalize(aud_key, scale_ak, gain_ak)
    normed_aq = normalize(aud_query, scale_aq, gain_aq)
    normed_vk = normalize(vid_key, scale_vk, gain_vk)

    def per_head(head_items):
        video_q, audio_k, audio_v, video_o, video_g, video_l, video_w, audio_q, video_k, video_v, audio_o, audio_g, audio_l, audio_w = head_items
        up_vq, up_ak, grad_av = one_direction(video_q, audio_k, audio_v, video_o, video_g, video_l, video_w)
        up_aq, up_vk, grad_vv = one_direction(audio_q, video_k, video_v, audio_o, audio_g, audio_l, audio_w)
        return (up_vq, up_ak, grad_av, up_aq, up_vk, grad_vv)
    up_vq, up_ak, grad_av, up_aq, up_vk, grad_vv = lax.map(per_head, (normed_vq, normed_ak, aud_value, vid_out, vid_grad, vid_lse, vid_mask, normed_aq, normed_vk, vid_value, aud_out, aud_grad, aud_lse, aud_mask))
    grad_vid_query = norm_backward(vid_query, scale_vq, gain_vq, up_vq)
    grad_aud_key = norm_backward(aud_key, scale_ak, gain_ak, up_ak)
    grad_aud_query = norm_backward(aud_query, scale_aq, gain_aq, up_aq)
    grad_vid_key = norm_backward(vid_key, scale_vk, gain_vk, up_vk)
    return (grad_vid_query, grad_vid_key, grad_vv.astype(jnp.bfloat16), grad_aud_query, grad_aud_key, grad_av.astype(jnp.bfloat16))
```

```python
import functools

import jax
import jax.numpy as jnp
from jax import lax
from jax.experimental import pallas as pl
from jax.experimental.pallas import tpu as pltpu
from jax.sharding import PartitionSpec as P

EPS = 1e-06
XS = 2
CORES = 2
CHUNK = 256
MESH = pl.DeviceIdType.MESH


def place():
    me = lax.axis_index("ctx")
    return me // (XS * CORES), lax.rem(me // CORES, XS), lax.rem(me, CORES)


def peer(z, x, c):
    return {"ctx": (z * XS + x) * CORES + c}


def enter(z, x, c, zs):
    barrier = pltpu.get_barrier_semaphore()
    targets = [peer(z, x, 1 - c), peer(z, 1 - x, c)]
    targets += [peer(lax.rem(z + d, zs), x, c) for d in range(1, zs)]
    for target in targets:
        pl.semaphore_signal(barrier, inc=1, device_id=target, device_id_type=MESH)
    pl.semaphore_wait(barrier, len(targets))


def gather_kernel(zs, big_ref, small_ref, big_out, small_out, z_send, z_recv, x_send, x_recv, c_send, c_recv, own_sem):
    z, x, c = place()
    enter(z, x, c, zs)
    pairs = ((big_ref, big_out), (small_ref, small_out))

    def slot(ref, k, zz, xx, cc):
        return ref.at[:, zz, xx, cc] if k == 0 else ref.at[zz, xx, cc]

    pending = []

    def z_copy(k, d):
        src, out = pairs[k]
        return pltpu.make_async_remote_copy(
            src_ref=src, dst_ref=slot(out, k, z, x, c), send_sem=z_send.at[k, d], recv_sem=z_recv.at[k, d],
            device_id=peer(lax.rem(z + d, zs), x, c), device_id_type=MESH)

    def x_copy(k, d):
        src, out = pairs[k]
        zz = lax.rem(z + zs - d, zs)
        there = slot(out, k, zz, x, c)
        return pltpu.make_async_remote_copy(
            src_ref=src if d == 0 else there, dst_ref=there, send_sem=x_send.at[k, d], recv_sem=x_recv.at[k, d],
            device_id=peer(z, 1 - x, c), device_id_type=MESH)

    def c_copy(k, d, side):
        src, out = pairs[k]
        zz = lax.rem(z + zs - d, zs)
        there = slot(out, k, zz, x if side == 0 else 1 - x, c)
        return pltpu.make_async_remote_copy(
            src_ref=src if d == 0 and side == 0 else there, dst_ref=there, send_sem=c_send.at[k, d, side],
            recv_sem=c_recv.at[k, d, side], device_id=peer(z, x, 1 - c), device_id_type=MESH)

    z_copies = [[z_copy(k, d) for k in range(2)] for d in range(1, zs)]
    x_copies = [[x_copy(k, d) for k in range(2)] for d in range(zs)]
    c_copies = [[[c_copy(k, d, side) for k in range(2)] for d in range(zs)] for side in range(2)]
    own = [pltpu.make_async_copy(pairs[k][0], slot(pairs[k][1], k, z, x, c), own_sem.at[k]) for k in range(2)]

    def start(group):
        for copy in group:
            copy.start()

    def arrive(group):
        for copy in group:
            copy.wait_recv()

    for group in z_copies:
        start(group)
    start(x_copies[0])
    start(c_copies[0][0])
    start(own)
    for d in range(1, zs):
        arrive(z_copies[d - 1])
        start(x_copies[d])
        start(c_copies[0][d])
    for d in range(zs):
        arrive(x_copies[d])
        start(c_copies[1][d])
    for side in range(2):
        for d in range(zs):
            arrive(c_copies[side][d])
    for copy in own:
        copy.wait()
    for group in z_copies + x_copies + c_copies[0] + c_copies[1]:
        for copy in group:
            copy.wait_send()


def gather(big, small, zs):
    rows, tokens, width = big.shape
    sems = lambda *shape: pltpu.SemaphoreType.DMA(shape)
    return pl.pallas_call(
        functools.partial(gather_kernel, zs),
        out_shape=(
            jax.ShapeDtypeStruct((rows, zs, XS, CORES, tokens, width), big.dtype),
            jax.ShapeDtypeStruct((zs, XS, CORES) + small.shape, small.dtype),
        ),
        in_specs=[pl.BlockSpec(memory_space=pltpu.VMEM)] * 2,
        out_specs=[pl.BlockSpec(memory_space=pltpu.VMEM)] * 2,
        scratch_shapes=[sems(2, zs), sems(2, zs), sems(2, zs), sems(2, zs), sems(2, zs, 2), sems(2, zs, 2), sems(2)],
        compiler_params=pltpu.CompilerParams(collective_id=0, has_side_effects=True, vmem_limit_bytes=48 << 20),
        name="gather_audio",
    )(big, small)


def scatter_kernel(zs, part_ref, out_ref, core_in, x_out, x_in, z_out, z_in, c_send, c_recv, x_send, x_recv, z_send, z_recv):
    z, x, c = place()
    enter(z, x, c, zs)
    order = list(range(1, zs)) + [0]
    target = [lax.rem(z + d, zs) for d in range(zs)]
    c_copies = [pltpu.make_async_remote_copy(
        src_ref=part_ref.at[:, target[d], :, 1 - c], dst_ref=core_in.at[d], send_sem=c_send.at[d], recv_sem=c_recv.at[d],
        device_id=peer(z, x, 1 - c), device_id_type=MESH) for d in range(zs)]
    x_copies = [pltpu.make_async_remote_copy(
        src_ref=x_out.at[d], dst_ref=x_in.at[d], send_sem=x_send.at[d], recv_sem=x_recv.at[d],
        device_id=peer(z, 1 - x, c), device_id_type=MESH) for d in range(zs)]
    z_copies = [pltpu.make_async_remote_copy(
        src_ref=z_out.at[d], dst_ref=z_in.at[d], send_sem=z_send.at[d], recv_sem=z_recv.at[d],
        device_id=peer(target[d], x, c), device_id_type=MESH) if d else None for d in range(zs)]
    for d in order:
        c_copies[d].start()

    def core_sum(d, side):
        return part_ref[:, target[d], side, c].astype(jnp.float32) + core_in[d, :, side].astype(jnp.float32)

    for d in order:
        c_copies[d].wait_recv()
        x_out[d] = core_sum(d, 1 - x).astype(x_out.dtype)
        x_copies[d].start()
    for d in order:
        x_copies[d].wait_recv()
        both = core_sum(d, x) + x_in[d].astype(jnp.float32)
        if d:
            z_out[d] = both.astype(z_out.dtype)
            z_copies[d].start()
        else:
            out_ref[...] = both
    for d in range(1, zs):
        z_copies[d].wait_recv()
        out_ref[...] += z_in[d].astype(jnp.float32)
    for d in range(zs):
        c_copies[d].wait_send()
        x_copies[d].wait_send()
        if d:
            z_copies[d].wait_send()


def scatter(part, zs):
    rows, _, _, _, tokens, width = part.shape
    sems = lambda: pltpu.SemaphoreType.DMA((zs,))
    block = lambda *lead: pltpu.VMEM(lead + (tokens, width), part.dtype)
    return pl.pallas_call(
        functools.partial(scatter_kernel, zs),
        out_shape=jax.ShapeDtypeStruct((rows, tokens, width), jnp.float32),
        in_specs=[pl.BlockSpec(memory_space=pltpu.VMEM)],
        out_specs=pl.BlockSpec(memory_space=pltpu.VMEM),
        scratch_shapes=[block(zs, rows, XS), block(zs, rows), block(zs, rows), block(zs, rows), block(zs, rows)]
        + [sems() for _ in range(6)],
        compiler_params=pltpu.CompilerParams(collective_id=1, has_side_effects=True, vmem_limit_bytes=56 << 20),
        name="scatter_audio",
    )(part)


def rows_dot(left, right):
    return lax.dot_general(left, right, (((1,), (1,)), ((), ())), preferred_element_type=jnp.float32)


def cols_dot(left, right):
    return lax.dot_general(left, right, (((0,), (0,)), ((), ())), preferred_element_type=jnp.float32)


def plain_dot(left, right):
    return lax.dot_general(left, right, (((1,), (0,)), ((), ())), preferred_element_type=jnp.float32)


def tile_terms(keys, values, queries, grads, lse, delta, words, first_key):
    nk, nw = keys.shape[0], words.shape[1]
    scale = keys.shape[1] ** (-0.5)
    key_of = lax.broadcasted_iota(jnp.int32, (nk, nw), 0) + first_key
    word_of = lax.broadcasted_iota(jnp.int32, (nk, nw), 1)
    spread = jnp.where(key_of // 8 == word_of, 1.0, 0.0).astype(jnp.bfloat16)
    spread_words = rows_dot(spread, words).astype(jnp.int32)
    shape = spread_words.shape
    bit = jnp.left_shift(1, lax.rem(lax.broadcasted_iota(jnp.int32, shape, 0), 8))
    keep = jnp.bitwise_and(spread_words, bit) != 0
    probs = jnp.exp(rows_dot(keys, queries) * scale - lse)
    dropped = jnp.where(keep, 2.0 * probs, 0.0).astype(jnp.bfloat16)
    prob_grad = jnp.where(keep, 2.0 * rows_dot(values, grads), 0.0)
    score_grad = (probs * (prob_grad - delta)).astype(jnp.bfloat16)
    return (
        plain_dot(dropped, grads),
        scale * plain_dot(score_grad, queries),
        scale * cols_dot(score_grad, keys),
    )


def attention_kernel(aud_ref, vq_ref, vk_ref, vv_ref, vg_ref, vl_ref, vd_ref, vw_ref, al_ref, ad_ref, aw_ref,
                     dvq_ref, dvk_ref, dvv_ref, part_ref):
    audio = aud_ref.shape[2]
    chunk = min(CHUNK, audio)
    vq, vk, vv, vg = vq_ref[0], vk_ref[0], vv_ref[0], vg_ref[0]
    vid_words = vw_ref[0].astype(jnp.float32).astype(jnp.bfloat16)
    for first in range(0, audio, chunk):
        rows = pl.ds(first, chunk)
        ak, av, aq, ag = (aud_ref[i, 0, rows, :] for i in range(4))
        value_grad, key_grad, query_grad = tile_terms(
            ak, av, vq, vg, vl_ref[0], vd_ref[0], vid_words, first)
        part_ref[0, 0, rows, :] = key_grad.astype(jnp.bfloat16)
        part_ref[1, 0, rows, :] = value_grad.astype(jnp.bfloat16)
        if first:
            dvq_ref[0] += query_grad
        else:
            dvq_ref[0] = query_grad
        aud_words = aw_ref[0, rows, :].astype(jnp.float32).astype(jnp.bfloat16)
        value_grad, key_grad, query_grad = tile_terms(
            vk, vv, aq, ag, al_ref[0, :, rows], ad_ref[0, :, rows], aud_words, 0)
        part_ref[2, 0, rows, :] = query_grad.astype(jnp.bfloat16)
        if first:
            dvk_ref[0] += key_grad
            dvv_ref[0] += value_grad
        else:
            dvk_ref[0] = key_grad
            dvv_ref[0] = value_grad


def attention(aud, vq, vk, vv, vg, vl, vd, vw, al, ad, aw):
    heads, video, width = vq.shape
    audio = aud.shape[2]
    rows = lambda a: pl.BlockSpec((1,) + a.shape[1:], lambda h: (h,) + (0,) * (a.ndim - 1))
    args = (vq, vk, vv, vg, vl, vd, vw, al, ad, aw)
    grad = jax.ShapeDtypeStruct((heads, video, width), jnp.float32)
    stack = lambda n: pl.BlockSpec((n, 1, audio, width), lambda h: (0, h, 0, 0))
    return pl.pallas_call(
        attention_kernel,
        grid=(heads,),
        out_shape=(grad, grad, grad, jax.ShapeDtypeStruct((3, heads, audio, width), jnp.bfloat16)),
        in_specs=[stack(4)] + [rows(a) for a in args],
        out_specs=(rows(vq), rows(vq), rows(vq), stack(3)),
        compiler_params=pltpu.CompilerParams(vmem_limit_bytes=48 << 20),
        name="attention_grads",
    )(aud, *args)


def square_sums(tokens):
    values = tokens.astype(jnp.float32)
    return jnp.sum(values * values, axis=(0, 2))


def normalize(tokens, scales, gain_rows):
    return (tokens.astype(jnp.float32) * scales[None, :, None] * gain_rows[:, None, :]).astype(jnp.bfloat16)


def norm_parts(tokens, scales, gain_rows, upstream):
    weighted = upstream * gain_rows[:, None, :]
    unit_rows = tokens.astype(jnp.float32) * scales[None, :, None]
    return (weighted, unit_rows, jnp.sum(weighted * unit_rows, axis=(0, 2)))


def norm_finish(weighted, unit_rows, scales, product, feature_count):
    mean_term = product / feature_count
    return (scales[None, :, None] * (weighted - unit_rows * mean_term[None, :, None])).astype(jnp.bfloat16)


def local(vid_query, vid_key, vid_value, vid_out, vid_grad, vid_lse, vid_mask, aud_query, aud_key, aud_value,
          aud_out, aud_grad, aud_lse, aud_mask, gain_vq, gain_ak, gain_aq, gain_vk):
    heads, video, width = vid_query.shape
    tokens = aud_key.shape[1]
    feature_count = lax.axis_size("head") * heads * width
    zs = lax.axis_size("ctx") // (XS * CORES)
    audio = tokens * lax.axis_size("ctx")
    sums = lax.psum(
        jnp.concatenate([square_sums(a) for a in (vid_query, vid_key, aud_query, aud_key)]), "head")
    scales = lax.rsqrt(sums / feature_count + EPS)
    scale_vq, scale_vk = scales[:video], scales[video:2 * video]
    scale_aq, scale_ak = scales[2 * video:2 * video + tokens], scales[2 * video + tokens:]
    video_delta = jnp.sum(vid_grad.astype(jnp.float32) * vid_out.astype(jnp.float32), axis=2)
    audio_delta = jnp.sum(aud_grad.astype(jnp.float32) * aud_out.astype(jnp.float32), axis=2)
    big = jnp.concatenate(
        [normalize(aud_key, scale_ak, gain_ak), aud_value, normalize(aud_query, scale_aq, gain_aq), aud_grad])
    small = jnp.pad(jnp.concatenate([aud_lse, audio_delta]), ((0, 0), (0, 128 - tokens)))
    big, small = gather(big, small, zs)
    big = big.reshape(4, heads, audio, width)
    small = small[..., :tokens].transpose(3, 0, 1, 2, 4).reshape(2, heads, 1, audio)
    up_vq, up_vk, up_vv, part = attention(
        big, normalize(vid_query, scale_vq, gain_vq), normalize(vid_key, scale_vk, gain_vk), vid_value, vid_grad,
        vid_lse[:, None], video_delta[:, None], vid_mask, small[0], small[1], aud_mask)
    sums = scatter(part.reshape(3 * heads, zs, XS, CORES, tokens, width), zs).reshape(3, heads, tokens, width)
    up_ak, up_av, up_aq = sums[0], sums[1], sums[2]
    parts = [
        norm_parts(vid_query, scale_vq, gain_vq, up_vq),
        norm_parts(vid_key, scale_vk, gain_vk, up_vk),
        norm_parts(aud_query, scale_aq, gain_aq, up_aq),
        norm_parts(aud_key, scale_ak, gain_ak, up_ak),
    ]
    product = lax.psum(jnp.concatenate([p[2] for p in parts]), "head")
    cuts = (0, video, 2 * video, 2 * video + tokens, 2 * video + 2 * tokens)
    done = [
        norm_finish(w, u, scales[lo:hi], product[lo:hi], feature_count)
        for (w, u, _), lo, hi in zip(parts, cuts[:-1], cuts[1:])
    ]
    return (done[0], done[1], up_vv.astype(jnp.bfloat16), done[2], done[3], up_av.astype(jnp.bfloat16))


def solution(mesh):
    rows = P("head", "ctx", None)
    line = P("head", "ctx")
    gain = P("head", None)
    return jax.shard_map(
        local,
        mesh=mesh,
        in_specs=(rows, rows, rows, rows, rows, line, rows, rows, rows, rows, rows, rows, line,
                  P("head", None, "ctx"), gain, gain, gain, gain),
        out_specs=(rows,) * 6,
        check_vma=False,
    )
```

```python
import functools

import jax
import jax.numpy as jnp
from jax import lax
from jax.experimental import pallas as pl
from jax.experimental.pallas import tpu as pltpu
from jax.sharding import PartitionSpec as P

EPS = 1e-06
XS = 2
CORES = 2
MESH = pl.DeviceIdType.MESH


def place():
    me = lax.axis_index("ctx")
    return me // (XS * CORES), lax.rem(me // CORES, XS), lax.rem(me, CORES)


def peer(z, x, c):
    return {"ctx": (z * XS + x) * CORES + c}


def enter(z, x, c, zs):
    barrier = pltpu.get_barrier_semaphore()
    targets = [peer(z, x, 1 - c), peer(z, 1 - x, c)]
    targets += [peer(lax.rem(z + d, zs), x, c) for d in range(1, zs)]
    for target in targets:
        pl.semaphore_signal(barrier, inc=1, device_id=target, device_id_type=MESH)
    pl.semaphore_wait(barrier, len(targets))


def rows_dot(left, right):
    return lax.dot_general(left, right, (((1,), (1,)), ((), ())), preferred_element_type=jnp.float32)


def cols_dot(left, right):
    return lax.dot_general(left, right, (((0,), (0,)), ((), ())), preferred_element_type=jnp.float32)


def plain_dot(left, right):
    return lax.dot_general(left, right, (((1,), (0,)), ((), ())), preferred_element_type=jnp.float32)


def tile_terms(keys, values, queries, grads, lse, delta, words, first_key):
    nk, nw = keys.shape[0], words.shape[1]
    scale = keys.shape[1] ** (-0.5)
    key_of = lax.broadcasted_iota(jnp.int32, (nk, nw), 0) + first_key
    word_of = lax.broadcasted_iota(jnp.int32, (nk, nw), 1)
    spread = jnp.where(key_of // 8 == word_of, 1.0, 0.0).astype(jnp.bfloat16)
    spread_words = rows_dot(spread, words).astype(jnp.int32)
    shape = spread_words.shape
    bit = jnp.left_shift(1, lax.rem(lax.broadcasted_iota(jnp.int32, shape, 0), 8))
    keep = jnp.bitwise_and(spread_words, bit) != 0
    probs = jnp.exp(rows_dot(keys, queries) * scale - lse)
    dropped = jnp.where(keep, 2.0 * probs, 0.0).astype(jnp.bfloat16)
    prob_grad = jnp.where(keep, 2.0 * rows_dot(values, grads), 0.0)
    score_grad = (probs * (prob_grad - delta)).astype(jnp.bfloat16)
    return (
        plain_dot(dropped, grads),
        scale * plain_dot(score_grad, queries),
        scale * cols_dot(score_grad, keys),
    )


def fused_kernel(zs, big_ref, small_ref, vq_ref, vk_ref, vv_ref, vg_ref, vl_ref, vd_ref, vw_ref, aw_ref,
                 dvq_ref, dvk_ref, dvv_ref, sum_ref,
                 big_out, small_out, part, core_in, x_out, x_in, z_out, z_in,
                 z_send, z_recv, x_send, x_recv, c_send, c_recv, own_sem,
                 pc_send, pc_recv, px_send, px_recv, pz_send, pz_recv):
    z, x, c = place()
    heads = vq_ref.shape[0]
    width = vq_ref.shape[2]
    chunk = XS * CORES * big_ref.shape[1]
    source = [lax.rem(z + zs - d, zs) for d in range(zs)]
    enter(z, x, c, zs)
    pairs = ((big_ref, big_out), (small_ref, small_out))

    def slot(k, zz, xx):
        out = pairs[k][1]
        return out.at[:, zz, xx, c] if k == 0 else out.at[zz, xx, c]

    def copies(here, there, send, recv, target):
        return [pltpu.make_async_remote_copy(
            src_ref=here(k), dst_ref=there(k), send_sem=send(k), recv_sem=recv(k), device_id=target,
            device_id_type=MESH) for k in range(2)]

    own_src = lambda k: pairs[k][0]
    z_copies, x_copies, c_copies = [None], [], [[], []]
    for d in range(zs):
        mine = lambda k, d=d: slot(k, source[d], x)
        other = lambda k, d=d: slot(k, source[d], 1 - x)
        src = mine if d else own_src
        if d:
            z_copies.append(copies(own_src, lambda k: slot(k, z, x), lambda k, d=d: z_send.at[k, d],
                                   lambda k, d=d: z_recv.at[k, d], peer(lax.rem(z + d, zs), x, c)))
        x_copies.append(copies(src, mine, lambda k, d=d: x_send.at[k, d], lambda k, d=d: x_recv.at[k, d],
                               peer(z, 1 - x, c)))
        for side, here, there in ((0, src, mine), (1, other, other)):
            c_copies[side].append(copies(here, there, lambda k, d=d, side=side: c_send.at[k, d, side],
                                         lambda k, d=d, side=side: c_recv.at[k, d, side], peer(z, x, 1 - c)))
    own = [pltpu.make_async_copy(pairs[k][0], slot(k, z, x), own_sem.at[k]) for k in range(2)]
    pc_copies = [pltpu.make_async_remote_copy(
        src_ref=part.at[d, :, :, 1 - c], dst_ref=core_in.at[d], send_sem=pc_send.at[d], recv_sem=pc_recv.at[d],
        device_id=peer(z, x, 1 - c), device_id_type=MESH) for d in range(zs)]
    px_copies = [pltpu.make_async_remote_copy(
        src_ref=x_out.at[d], dst_ref=x_in.at[d], send_sem=px_send.at[d], recv_sem=px_recv.at[d],
        device_id=peer(z, 1 - x, c), device_id_type=MESH) for d in range(zs)]
    pz_copies = [None] + [pltpu.make_async_remote_copy(
        src_ref=z_out.at[d], dst_ref=z_in.at[d], send_sem=pz_send.at[d], recv_sem=pz_recv.at[d],
        device_id=peer(source[d], x, c), device_id_type=MESH) for d in range(1, zs)]

    def start(group):
        for copy in group:
            copy.start()

    def arrive(group):
        for copy in group:
            copy.wait_recv()

    def left(group):
        for copy in group:
            copy.wait_send()

    def compute(d):
        zz = source[d]
        rows = pl.ds(pl.multiple_of(zz * chunk, chunk), chunk)

        def head(h, carry):
            ak, av, aq, ag = (big_out[i * heads + h, zz].reshape(chunk, width) for i in range(4))
            lines = lambda i: sum(
                small_out[zz, xx, cc, pl.ds(i * heads + h, 1), :] for xx in range(XS) for cc in range(CORES))
            value_grad, key_grad, query_grad = tile_terms(
                ak, av, vq_ref[h], vg_ref[h], vl_ref[h], vd_ref[h],
                vw_ref[h].astype(jnp.float32).astype(jnp.bfloat16), zz * chunk)
            aud_words = aw_ref[h, rows, :].astype(jnp.float32).astype(jnp.bfloat16)
            vid_value_grad, vid_key_grad, aud_query_grad = tile_terms(
                vk_ref[h], vv_ref[h], aq, ag, lines(0), lines(1), aud_words, 0)
            for i, total in enumerate((key_grad, value_grad, aud_query_grad)):
                part[d, i * heads + h] = total.astype(part.dtype).reshape(part.shape[2:])
            if d:
                dvq_ref[h] += query_grad
                dvk_ref[h] += vid_key_grad
                dvv_ref[h] += vid_value_grad
            else:
                dvq_ref[h] = query_grad
                dvk_ref[h] = vid_key_grad
                dvv_ref[h] = vid_value_grad
            return carry

        lax.fori_loop(0, heads, head, 0)

    def core_sum(d, side):
        return part[d, :, side, c].astype(jnp.float32) + core_in[d, :, side].astype(jnp.float32)

    def to_x(d):
        pc_copies[d].wait_recv()
        x_out[d] = core_sum(d, 1 - x).astype(x_out.dtype)
        px_copies[d].start()

    def to_z(d):
        px_copies[d].wait_recv()
        both = core_sum(d, x) + x_in[d].astype(jnp.float32)
        if d:
            z_out[d] = both.astype(z_out.dtype)
            pz_copies[d].start()
        else:
            sum_ref[...] = both

    start(z_copies[1])
    start(x_copies[0])
    start(c_copies[0][0])
    start(own)
    for copy in own:
        copy.wait()
    for d in range(zs):
        if d + 1 < zs:
            if d + 2 < zs:
                left(z_copies[d + 1])
                start(z_copies[d + 2])
            arrive(z_copies[d + 1])
            start(x_copies[d + 1])
            start(c_copies[0][d + 1])
        arrive(x_copies[d])
        start(c_copies[1][d])
        if d > 0:
            to_x(d - 1)
        if d > 1:
            to_z(d - 2)
        arrive(c_copies[0][d])
        arrive(c_copies[1][d])
        compute(d)
        pc_copies[d].start()
    to_x(zs - 1)
    for d in range(max(zs - 2, 0), zs):
        to_z(d)
    for d in range(1, zs):
        pz_copies[d].wait_recv()
        sum_ref[...] += z_in[d].astype(jnp.float32)
    left(z_copies[zs - 1])
    for d in range(zs):
        left(x_copies[d])
        left(c_copies[0][d])
        left(c_copies[1][d])
        pc_copies[d].wait_send()
        px_copies[d].wait_send()
        if d:
            pz_copies[d].wait_send()


def fused(zs, big, small, vq, vk, vv, vg, vl, vd, vw, aw):
    rows, tokens, width = big.shape
    heads = vq.shape[0]
    lines = 3 * heads
    sems = lambda *shape: pltpu.SemaphoreType.DMA(shape)
    block = lambda *lead: pltpu.VMEM((zs, lines) + lead + (tokens, width), jnp.bfloat16)
    grad = jax.ShapeDtypeStruct(vq.shape, jnp.float32)
    vmem = pl.BlockSpec(memory_space=pltpu.VMEM)
    return pl.pallas_call(
        functools.partial(fused_kernel, zs),
        out_shape=(grad, grad, grad, jax.ShapeDtypeStruct((lines, tokens, width), jnp.float32)),
        in_specs=[vmem] * 10,
        out_specs=[vmem] * 4,
        scratch_shapes=[
            pltpu.VMEM((rows, zs, XS, CORES, tokens, width), big.dtype),
            pltpu.VMEM((zs, XS, CORES) + small.shape, small.dtype),
            block(XS, CORES), block(XS), block(), block(), block(), block(),
            sems(2, zs), sems(2, zs), sems(2, zs), sems(2, zs), sems(2, zs, 2), sems(2, zs, 2), sems(2),
        ] + [sems(zs) for _ in range(6)],
        compiler_params=pltpu.CompilerParams(collective_id=0, has_side_effects=True, vmem_limit_bytes=56 << 20),
        name="fused_grads",
    )(big, small, vq, vk, vv, vg, vl, vd, vw, aw)


def square_sums(tokens):
    values = tokens.astype(jnp.float32)
    return jnp.sum(values * values, axis=(0, 2))


def normalize(tokens, scales, gain_rows):
    return (tokens.astype(jnp.float32) * scales[None, :, None] * gain_rows[:, None, :]).astype(jnp.bfloat16)


def norm_parts(tokens, scales, gain_rows, upstream):
    weighted = upstream * gain_rows[:, None, :]
    unit_rows = tokens.astype(jnp.float32) * scales[None, :, None]
    return (weighted, unit_rows, jnp.sum(weighted * unit_rows, axis=(0, 2)))


def norm_finish(weighted, unit_rows, scales, product, feature_count):
    mean_term = product / feature_count
    return (scales[None, :, None] * (weighted - unit_rows * mean_term[None, :, None])).astype(jnp.bfloat16)


def local(vid_query, vid_key, vid_value, vid_out, vid_grad, vid_lse, vid_mask, aud_query, aud_key, aud_value,
          aud_out, aud_grad, aud_lse, aud_mask, gain_vq, gain_ak, gain_aq, gain_vk):
    heads, video, width = vid_query.shape
    tokens = aud_key.shape[1]
    feature_count = lax.axis_size("head") * heads * width
    zs = lax.axis_size("ctx") // (XS * CORES)
    sums = lax.psum(
        jnp.concatenate([square_sums(a) for a in (vid_query, vid_key, aud_query, aud_key)]), "head")
    scales = lax.rsqrt(sums / feature_count + EPS)
    scale_vq, scale_vk = scales[:video], scales[video:2 * video]
    scale_aq, scale_ak = scales[2 * video:2 * video + tokens], scales[2 * video + tokens:]
    video_delta = jnp.sum(vid_grad.astype(jnp.float32) * vid_out.astype(jnp.float32), axis=2)
    audio_delta = jnp.sum(aud_grad.astype(jnp.float32) * aud_out.astype(jnp.float32), axis=2)
    big = jnp.concatenate(
        [normalize(aud_key, scale_ak, gain_ak), aud_value, normalize(aud_query, scale_aq, gain_aq), aud_grad])
    near = XS * CORES
    lane_owner = jnp.arange(near * tokens) // tokens
    small = jnp.where(
        lane_owner[None] == lax.rem(lax.axis_index("ctx"), near),
        jnp.tile(jnp.concatenate([aud_lse, audio_delta]), (1, near)), 0.0)
    up_vq, up_vk, up_vv, sums = fused(
        zs, big, small, normalize(vid_query, scale_vq, gain_vq), normalize(vid_key, scale_vk, gain_vk), vid_value,
        vid_grad, vid_lse[:, None], video_delta[:, None], vid_mask, aud_mask)
    sums = sums.reshape(3, heads, tokens, width)
    up_ak, up_av, up_aq = sums[0], sums[1], sums[2]
    parts = [
        norm_parts(vid_query, scale_vq, gain_vq, up_vq),
        norm_parts(vid_key, scale_vk, gain_vk, up_vk),
        norm_parts(aud_query, scale_aq, gain_aq, up_aq),
        norm_parts(aud_key, scale_ak, gain_ak, up_ak),
    ]
    product = lax.psum(jnp.concatenate([p[2] for p in parts]), "head")
    cuts = (0, video, 2 * video, 2 * video + tokens, 2 * video + 2 * tokens)
    done = [
        norm_finish(w, u, scales[lo:hi], product[lo:hi], feature_count)
        for (w, u, _), lo, hi in zip(parts, cuts[:-1], cuts[1:])
    ]
    return (done[0], done[1], up_vv.astype(jnp.bfloat16), done[2], done[3], up_av.astype(jnp.bfloat16))


def solution(mesh):
    rows = P("head", "ctx", None)
    line = P("head", "ctx")
    gain = P("head", None)
    return jax.shard_map(
        local,
        mesh=mesh,
        in_specs=(rows, rows, rows, rows, rows, line, rows, rows, rows, rows, rows, rows, line,
                  P("head", None, "ctx"), gain, gain, gain, gain),
        out_specs=(rows,) * 6,
        check_vma=False,
    )
```

```python
import functools

import jax
import jax.numpy as jnp
from jax import lax
from jax.experimental import pallas as pl
from jax.experimental.pallas import tpu as pltpu
from jax.sharding import PartitionSpec as P

EPS = 1e-06
XS = 2
CORES = 2
MESH = pl.DeviceIdType.MESH


def place():
    me = lax.axis_index("ctx")
    return me // (XS * CORES), lax.rem(me // CORES, XS), lax.rem(me, CORES)


def peer(z, x, c):
    return {"ctx": (z * XS + x) * CORES + c}


def enter(z, x, c, zs):
    barrier = pltpu.get_barrier_semaphore()
    targets = [peer(z, x, 1 - c), peer(z, 1 - x, c)]
    targets += [peer(lax.rem(z + d, zs), x, c) for d in range(1, zs)]
    for target in targets:
        pl.semaphore_signal(barrier, inc=1, device_id=target, device_id_type=MESH)
    pl.semaphore_wait(barrier, len(targets))


def rows_dot(left, right):
    return lax.dot_general(left, right, (((1,), (1,)), ((), ())), preferred_element_type=jnp.float32)


def cols_dot(left, right):
    return lax.dot_general(left, right, (((0,), (0,)), ((), ())), preferred_element_type=jnp.float32)


def plain_dot(left, right):
    return lax.dot_general(left, right, (((1,), (0,)), ((), ())), preferred_element_type=jnp.float32)


def tile_terms(keys, values, queries, grads, lse, delta, words, first_key):
    nk, nw = keys.shape[0], words.shape[1]
    scale = keys.shape[1] ** (-0.5)
    key_of = lax.broadcasted_iota(jnp.int32, (nk, nw), 0) + first_key
    word_of = lax.broadcasted_iota(jnp.int32, (nk, nw), 1)
    spread = jnp.where(key_of // 8 == word_of, 1.0, 0.0).astype(jnp.bfloat16)
    spread_words = rows_dot(spread, words).astype(jnp.int32)
    shape = spread_words.shape
    bit = jnp.left_shift(1, lax.rem(lax.broadcasted_iota(jnp.int32, shape, 0), 8))
    keep = jnp.bitwise_and(spread_words, bit) != 0
    probs = jnp.exp(rows_dot(keys, queries) * scale - lse)
    dropped = jnp.where(keep, 2.0 * probs, 0.0).astype(jnp.bfloat16)
    prob_grad = jnp.where(keep, 2.0 * rows_dot(values, grads), 0.0)
    score_grad = (probs * (prob_grad - delta)).astype(jnp.bfloat16)
    return (
        plain_dot(dropped, grads),
        scale * plain_dot(score_grad, queries),
        scale * cols_dot(score_grad, keys),
    )


def fused_kernel(zs, big_ref, small_ref, vq_ref, vk_ref, vv_ref, vg_ref, vl_ref, vd_ref, vw_ref, aw_ref,
                 dvq_ref, dvk_ref, dvv_ref, sum_ref,
                 big_out, small_out, part, core_in, x_out, x_in, z_out, z_in,
                 z_send, z_recv, x_send, x_recv, c_send, c_recv, own_sem,
                 pc_send, pc_recv, px_send, px_recv, pz_send, pz_recv):
    z, x, c = place()
    heads = vq_ref.shape[0]
    width = vq_ref.shape[2]
    chunk = XS * CORES * big_ref.shape[1]
    source = [lax.rem(z + zs - d, zs) for d in range(zs)]
    enter(z, x, c, zs)
    pairs = ((big_ref, big_out), (small_ref, small_out))

    def slot(k, zz, xx):
        out = pairs[k][1]
        return out.at[:, zz, xx, c] if k == 0 else out.at[zz, xx, c]

    def copies(here, there, send, recv, target):
        return [pltpu.make_async_remote_copy(
            src_ref=here(k), dst_ref=there(k), send_sem=send(k), recv_sem=recv(k), device_id=target,
            device_id_type=MESH) for k in range(2)]

    own_src = lambda k: pairs[k][0]
    z_copies, x_copies, c_copies = [None], [], [[], []]
    for d in range(zs):
        mine = lambda k, d=d: slot(k, source[d], x)
        other = lambda k, d=d: slot(k, source[d], 1 - x)
        src = mine if d else own_src
        if d:
            z_copies.append(copies(own_src, lambda k: slot(k, z, x), lambda k, d=d: z_send.at[k, d],
                                   lambda k, d=d: z_recv.at[k, d], peer(lax.rem(z + d, zs), x, c)))
        x_copies.append(copies(src, mine, lambda k, d=d: x_send.at[k, d], lambda k, d=d: x_recv.at[k, d],
                               peer(z, 1 - x, c)))
        for side, here, there in ((0, src, mine), (1, other, other)):
            c_copies[side].append(copies(here, there, lambda k, d=d, side=side: c_send.at[k, d, side],
                                         lambda k, d=d, side=side: c_recv.at[k, d, side], peer(z, x, 1 - c)))
    own = [pltpu.make_async_copy(pairs[k][0], slot(k, z, x), own_sem.at[k]) for k in range(2)]
    pc_copies = [pltpu.make_async_remote_copy(
        src_ref=part.at[d, :, :, 1 - c], dst_ref=core_in.at[d], send_sem=pc_send.at[d], recv_sem=pc_recv.at[d],
        device_id=peer(z, x, 1 - c), device_id_type=MESH) for d in range(zs)]
    px_copies = [pltpu.make_async_remote_copy(
        src_ref=x_out.at[d], dst_ref=x_in.at[d], send_sem=px_send.at[d], recv_sem=px_recv.at[d],
        device_id=peer(z, 1 - x, c), device_id_type=MESH) for d in range(zs)]
    pz_copies = [None] + [pltpu.make_async_remote_copy(
        src_ref=z_out.at[d], dst_ref=z_in.at[d], send_sem=pz_send.at[d], recv_sem=pz_recv.at[d],
        device_id=peer(source[d], x, c), device_id_type=MESH) for d in range(1, zs)]

    def start(group):
        for copy in group:
            copy.start()

    def arrive(group):
        for copy in group:
            copy.wait_recv()

    def left(group):
        for copy in group:
            copy.wait_send()

    def compute(d):
        zz = source[d]
        rows = pl.ds(pl.multiple_of(zz * chunk, chunk), chunk)

        def head(h, carry):
            ak, av, aq, ag = (big_out[i * heads + h, zz].reshape(chunk, width) for i in range(4))
            lines = lambda i: sum(
                small_out[zz, xx, cc, pl.ds(i * heads + h, 1), :] for xx in range(XS) for cc in range(CORES))
            value_grad, key_grad, query_grad = tile_terms(
                ak, av, vq_ref[h], vg_ref[h], vl_ref[h], vd_ref[h],
                vw_ref[h].astype(jnp.float32).astype(jnp.bfloat16), zz * chunk)
            aud_words = aw_ref[h, rows, :].astype(jnp.float32).astype(jnp.bfloat16)
            vid_value_grad, vid_key_grad, aud_query_grad = tile_terms(
                vk_ref[h], vv_ref[h], aq, ag, lines(0), lines(1), aud_words, 0)
            for i, total in enumerate((key_grad, value_grad, aud_query_grad)):
                part[d, i * heads + h] = total.astype(part.dtype).reshape(part.shape[2:])
            if d:
                dvq_ref[h] += query_grad
                dvk_ref[h] += vid_key_grad
                dvv_ref[h] += vid_value_grad
            else:
                dvq_ref[h] = query_grad
                dvk_ref[h] = vid_key_grad
                dvv_ref[h] = vid_value_grad
            return carry

        lax.fori_loop(0, heads, head, 0)

    def core_sum(d, side):
        return part[d, :, side, c].astype(jnp.float32) + core_in[d, :, side].astype(jnp.float32)

    def to_x(d):
        pc_copies[d].wait_recv()
        x_out[d] = core_sum(d, 1 - x).astype(x_out.dtype)
        px_copies[d].start()

    def to_z(d):
        px_copies[d].wait_recv()
        both = core_sum(d, x) + x_in[d].astype(jnp.float32)
        if d:
            z_out[d] = both.astype(z_out.dtype)
            pz_copies[d].start()
        else:
            sum_ref[...] = both

    start(z_copies[1])
    start(x_copies[0])
    start(c_copies[0][0])
    start(own)
    for copy in own:
        copy.wait()

    def bring(d):
        if d + 1 < zs:
            left(z_copies[d])
            start(z_copies[d + 1])
        arrive(z_copies[d])
        start(x_copies[d])
        start(c_copies[0][d])

    for d in range(zs):
        if 0 < d < zs - 1:
            bring(d + 1)
        arrive(x_copies[d])
        start(c_copies[1][d])
        arrive(c_copies[0][d])
        arrive(c_copies[1][d])
        compute(d)
        pc_copies[d].start()
        if d == 0:
            bring(1)
        to_x(d)
        if d > 0:
            to_z(d - 1)
    to_z(zs - 1)
    for d in range(1, zs):
        pz_copies[d].wait_recv()
        sum_ref[...] += z_in[d].astype(jnp.float32)
    left(z_copies[zs - 1])
    for d in range(zs):
        left(x_copies[d])
        left(c_copies[0][d])
        left(c_copies[1][d])
        pc_copies[d].wait_send()
        px_copies[d].wait_send()
        if d:
            pz_copies[d].wait_send()


def fused(zs, big, small, vq, vk, vv, vg, vl, vd, vw, aw):
    rows, tokens, width = big.shape
    heads = vq.shape[0]
    lines = 3 * heads
    sems = lambda *shape: pltpu.SemaphoreType.DMA(shape)
    block = lambda *lead: pltpu.VMEM((zs, lines) + lead + (tokens, width), jnp.bfloat16)
    grad = jax.ShapeDtypeStruct(vq.shape, jnp.float32)
    vmem = pl.BlockSpec(memory_space=pltpu.VMEM)
    return pl.pallas_call(
        functools.partial(fused_kernel, zs),
        out_shape=(grad, grad, grad, jax.ShapeDtypeStruct((lines, tokens, width), jnp.float32)),
        in_specs=[vmem] * 10,
        out_specs=[vmem] * 4,
        scratch_shapes=[
            pltpu.VMEM((rows, zs, XS, CORES, tokens, width), big.dtype),
            pltpu.VMEM((zs, XS, CORES) + small.shape, small.dtype),
            block(XS, CORES), block(XS), block(), block(), block(), block(),
            sems(2, zs), sems(2, zs), sems(2, zs), sems(2, zs), sems(2, zs, 2), sems(2, zs, 2), sems(2),
        ] + [sems(zs) for _ in range(6)],
        compiler_params=pltpu.CompilerParams(collective_id=0, has_side_effects=True, vmem_limit_bytes=56 << 20),
        name="fused_grads",
    )(big, small, vq, vk, vv, vg, vl, vd, vw, aw)


def square_sums(tokens):
    values = tokens.astype(jnp.float32)
    return jnp.sum(values * values, axis=(0, 2))


def normalize(tokens, scales, gain_rows):
    return (tokens.astype(jnp.float32) * scales[None, :, None] * gain_rows[:, None, :]).astype(jnp.bfloat16)


def norm_parts(tokens, scales, gain_rows, upstream):
    weighted = upstream * gain_rows[:, None, :]
    unit_rows = tokens.astype(jnp.float32) * scales[None, :, None]
    return (weighted, unit_rows, jnp.sum(weighted * unit_rows, axis=(0, 2)))


def norm_finish(weighted, unit_rows, scales, product, feature_count):
    mean_term = product / feature_count
    return (scales[None, :, None] * (weighted - unit_rows * mean_term[None, :, None])).astype(jnp.bfloat16)


def local(vid_query, vid_key, vid_value, vid_out, vid_grad, vid_lse, vid_mask, aud_query, aud_key, aud_value,
          aud_out, aud_grad, aud_lse, aud_mask, gain_vq, gain_ak, gain_aq, gain_vk):
    heads, video, width = vid_query.shape
    tokens = aud_key.shape[1]
    feature_count = lax.axis_size("head") * heads * width
    zs = lax.axis_size("ctx") // (XS * CORES)
    sums = lax.psum(
        jnp.concatenate([square_sums(a) for a in (vid_query, vid_key, aud_query, aud_key)]), "head")
    scales = lax.rsqrt(sums / feature_count + EPS)
    scale_vq, scale_vk = scales[:video], scales[video:2 * video]
    scale_aq, scale_ak = scales[2 * video:2 * video + tokens], scales[2 * video + tokens:]
    video_delta = jnp.sum(vid_grad.astype(jnp.float32) * vid_out.astype(jnp.float32), axis=2)
    audio_delta = jnp.sum(aud_grad.astype(jnp.float32) * aud_out.astype(jnp.float32), axis=2)
    big = jnp.concatenate(
        [normalize(aud_key, scale_ak, gain_ak), aud_value, normalize(aud_query, scale_aq, gain_aq), aud_grad])
    near = XS * CORES
    lane_owner = jnp.arange(near * tokens) // tokens
    small = jnp.where(
        lane_owner[None] == lax.rem(lax.axis_index("ctx"), near),
        jnp.tile(jnp.concatenate([aud_lse, audio_delta]), (1, near)), 0.0)
    up_vq, up_vk, up_vv, sums = fused(
        zs, big, small, normalize(vid_query, scale_vq, gain_vq), normalize(vid_key, scale_vk, gain_vk), vid_value,
        vid_grad, vid_lse[:, None], video_delta[:, None], vid_mask, aud_mask)
    sums = sums.reshape(3, heads, tokens, width)
    up_ak, up_av, up_aq = sums[0], sums[1], sums[2]
    parts = [
        norm_parts(vid_query, scale_vq, gain_vq, up_vq),
        norm_parts(vid_key, scale_vk, gain_vk, up_vk),
        norm_parts(aud_query, scale_aq, gain_aq, up_aq),
        norm_parts(aud_key, scale_ak, gain_ak, up_ak),
    ]
    product = lax.psum(jnp.concatenate([p[2] for p in parts]), "head")
    cuts = (0, video, 2 * video, 2 * video + tokens, 2 * video + 2 * tokens)
    done = [
        norm_finish(w, u, scales[lo:hi], product[lo:hi], feature_count)
        for (w, u, _), lo, hi in zip(parts, cuts[:-1], cuts[1:])
    ]
    return (done[0], done[1], up_vv.astype(jnp.bfloat16), done[2], done[3], up_av.astype(jnp.bfloat16))


def solution(mesh):
    rows = P("head", "ctx", None)
    line = P("head", "ctx")
    gain = P("head", None)
    return jax.shard_map(
        local,
        mesh=mesh,
        in_specs=(rows, rows, rows, rows, rows, line, rows, rows, rows, rows, rows, rows, line,
                  P("head", None, "ctx"), gain, gain, gain, gain),
        out_specs=(rows,) * 6,
        check_vma=False,
    )
```

```python
import functools

import jax
import jax.numpy as jnp
from jax import lax
from jax.experimental import pallas as pl
from jax.experimental.pallas import tpu as pltpu
from jax.sharding import PartitionSpec as P

EPS = 1e-06
XS = 2
CORES = 2
MESH = pl.DeviceIdType.MESH


def place():
    me = lax.axis_index("ctx")
    return me // (XS * CORES), lax.rem(me // CORES, XS), lax.rem(me, CORES)


def peer(z, x, c):
    return {"ctx": (z * XS + x) * CORES + c}


def enter(z, x, c, zs):
    barrier = pltpu.get_barrier_semaphore()
    targets = [peer(z, x, 1 - c), peer(z, 1 - x, c)]
    targets += [peer(lax.rem(z + d, zs), x, c) for d in range(1, zs)]
    for target in targets:
        pl.semaphore_signal(barrier, inc=1, device_id=target, device_id_type=MESH)
    pl.semaphore_wait(barrier, len(targets))


def rows_dot(left, right):
    return lax.dot_general(left, right, (((1,), (1,)), ((), ())), preferred_element_type=jnp.float32)


def cols_dot(left, right):
    return lax.dot_general(left, right, (((0,), (0,)), ((), ())), preferred_element_type=jnp.float32)


def plain_dot(left, right):
    return lax.dot_general(left, right, (((1,), (0,)), ((), ())), preferred_element_type=jnp.float32)


def tile_terms(keys, values, queries, grads, lse, delta, words, first_key):
    nk, nw = keys.shape[0], words.shape[1]
    scale = keys.shape[1] ** (-0.5)
    key_of = lax.broadcasted_iota(jnp.int32, (nk, nw), 0) + first_key
    word_of = lax.broadcasted_iota(jnp.int32, (nk, nw), 1)
    spread = jnp.where(key_of // 8 == word_of, 1.0, 0.0).astype(jnp.bfloat16)
    spread_words = rows_dot(spread, words).astype(jnp.int32)
    shape = spread_words.shape
    bit = jnp.left_shift(1, lax.rem(lax.broadcasted_iota(jnp.int32, shape, 0), 8))
    keep = jnp.bitwise_and(spread_words, bit) != 0
    probs = jnp.exp(rows_dot(keys, queries) * scale - lse)
    dropped = jnp.where(keep, 2.0 * probs, 0.0).astype(jnp.bfloat16)
    prob_grad = jnp.where(keep, 2.0 * rows_dot(values, grads), 0.0)
    score_grad = (probs * (prob_grad - delta)).astype(jnp.bfloat16)
    return (
        plain_dot(dropped, grads),
        scale * plain_dot(score_grad, queries),
        scale * cols_dot(score_grad, keys),
    )


def fused_kernel(zs, big_ref, small_ref, vq_ref, vk_ref, vv_ref, vg_ref, vl_ref, vd_ref, vw_ref, aw_ref,
                 dvq_ref, dvk_ref, dvv_ref, sum_ref,
                 big_out, small_out, part, core_in, x_out, x_in, z_out, z_in,
                 z_send, z_recv, x_send, x_recv, c_send, c_recv, own_sem,
                 pc_send, pc_recv, px_send, px_recv, pz_send, pz_recv):
    z, x, c = place()
    heads = vq_ref.shape[0]
    width = vq_ref.shape[2]
    chunk = XS * CORES * big_ref.shape[1]
    source = [lax.rem(z + zs - d, zs) for d in range(zs)]
    enter(z, x, c, zs)
    pairs = ((big_ref, big_out), (small_ref, small_out))

    def slot(k, zz, xx):
        out = pairs[k][1]
        return out.at[:, zz, xx, c] if k == 0 else out.at[zz, xx, c]

    def copies(here, there, send, recv, target):
        return [pltpu.make_async_remote_copy(
            src_ref=here(k), dst_ref=there(k), send_sem=send(k), recv_sem=recv(k), device_id=target,
            device_id_type=MESH) for k in range(2)]

    own_src = lambda k: pairs[k][0]
    z_copies, x_copies, c_copies = [None], [], [[], []]
    for d in range(zs):
        mine = lambda k, d=d: slot(k, source[d], x)
        other = lambda k, d=d: slot(k, source[d], 1 - x)
        src = mine if d else own_src
        if d:
            z_copies.append(copies(own_src, lambda k: slot(k, z, x), lambda k, d=d: z_send.at[k, d],
                                   lambda k, d=d: z_recv.at[k, d], peer(lax.rem(z + d, zs), x, c)))
        x_copies.append(copies(src, mine, lambda k, d=d: x_send.at[k, d], lambda k, d=d: x_recv.at[k, d],
                               peer(z, 1 - x, c)))
        for side, here, there in ((0, src, mine), (1, other, other)):
            c_copies[side].append(copies(here, there, lambda k, d=d, side=side: c_send.at[k, d, side],
                                         lambda k, d=d, side=side: c_recv.at[k, d, side], peer(z, x, 1 - c)))
    own = [pltpu.make_async_copy(pairs[k][0], slot(k, z, x), own_sem.at[k]) for k in range(2)]
    pc_copies = [pltpu.make_async_remote_copy(
        src_ref=part.at[d, :, :, 1 - c], dst_ref=core_in.at[d], send_sem=pc_send.at[d], recv_sem=pc_recv.at[d],
        device_id=peer(z, x, 1 - c), device_id_type=MESH) for d in range(zs)]
    px_copies = [pltpu.make_async_remote_copy(
        src_ref=x_out.at[d], dst_ref=x_in.at[d], send_sem=px_send.at[d], recv_sem=px_recv.at[d],
        device_id=peer(z, 1 - x, c), device_id_type=MESH) for d in range(zs)]
    pz_copies = [None] + [pltpu.make_async_remote_copy(
        src_ref=z_out.at[d], dst_ref=z_in.at[d], send_sem=pz_send.at[d], recv_sem=pz_recv.at[d],
        device_id=peer(source[d], x, c), device_id_type=MESH) for d in range(1, zs)]

    def start(group):
        for copy in group:
            copy.start()

    def arrive(group):
        for copy in group:
            copy.wait_recv()

    def left(group):
        for copy in group:
            copy.wait_send()

    def compute(d):
        zz = source[d]
        rows = pl.ds(pl.multiple_of(zz * chunk, chunk), chunk)

        def head(h, carry):
            ak, av, aq, ag = (big_out[i * heads + h, zz].reshape(chunk, width) for i in range(4))
            lines = lambda i: sum(
                small_out[zz, xx, cc, pl.ds(i * heads + h, 1), :] for xx in range(XS) for cc in range(CORES))
            value_grad, key_grad, query_grad = tile_terms(
                ak, av, vq_ref[h], vg_ref[h], vl_ref[h], vd_ref[h],
                vw_ref[h].astype(jnp.float32).astype(jnp.bfloat16), zz * chunk)
            aud_words = aw_ref[h, rows, :].astype(jnp.float32).astype(jnp.bfloat16)
            vid_value_grad, vid_key_grad, aud_query_grad = tile_terms(
                vk_ref[h], vv_ref[h], aq, ag, lines(0), lines(1), aud_words, 0)
            for i, total in enumerate((key_grad, value_grad, aud_query_grad)):
                part[d, i * heads + h] = total.astype(part.dtype).reshape(part.shape[2:])
            if d:
                dvq_ref[h] += query_grad
                dvk_ref[h] += vid_key_grad
                dvv_ref[h] += vid_value_grad
            else:
                dvq_ref[h] = query_grad
                dvk_ref[h] = vid_key_grad
                dvv_ref[h] = vid_value_grad
            return carry

        lax.fori_loop(0, heads, head, 0)

    def core_sum(d, side):
        return part[d, :, side, c].astype(jnp.float32) + core_in[d, :, side].astype(jnp.float32)

    def to_x(d):
        pc_copies[d].wait_recv()
        x_out[d] = core_sum(d, 1 - x).astype(x_out.dtype)
        px_copies[d].start()

    def to_z(d):
        px_copies[d].wait_recv()
        both = core_sum(d, x) + x_in[d].astype(jnp.float32)
        if d:
            z_out[d] = both.astype(z_out.dtype)
            pz_copies[d].start()
        else:
            sum_ref[...] = both

    def ready(d):
        arrive(x_copies[d])
        start(c_copies[1][d])
        arrive(c_copies[0][d])
        arrive(c_copies[1][d])

    start(x_copies[0])
    for d in range(1, zs):
        start(z_copies[d])
    start(c_copies[0][0])
    start(own)
    for copy in own:
        copy.wait()
    ready(0)
    compute(0)
    pc_copies[0].start()
    for d in range(1, zs):
        arrive(z_copies[d])
        start(x_copies[d])
        start(c_copies[0][d])
    for d in range(1, zs):
        ready(d)
        compute(d)
        pc_copies[d].start()
        to_x(d)
        if d > 1:
            to_z(d - 1)
    to_z(zs - 1)
    to_x(0)
    to_z(0)
    for d in range(1, zs):
        pz_copies[d].wait_recv()
        sum_ref[...] += z_in[d].astype(jnp.float32)
    for d in range(zs):
        if d:
            left(z_copies[d])
        left(x_copies[d])
        left(c_copies[0][d])
        left(c_copies[1][d])
        pc_copies[d].wait_send()
        px_copies[d].wait_send()
        if d:
            pz_copies[d].wait_send()


def fused(zs, big, small, vq, vk, vv, vg, vl, vd, vw, aw):
    rows, tokens, width = big.shape
    heads = vq.shape[0]
    lines = 3 * heads
    sems = lambda *shape: pltpu.SemaphoreType.DMA(shape)
    block = lambda *lead: pltpu.VMEM((zs, lines) + lead + (tokens, width), jnp.bfloat16)
    grad = jax.ShapeDtypeStruct(vq.shape, jnp.float32)
    vmem = pl.BlockSpec(memory_space=pltpu.VMEM)
    return pl.pallas_call(
        functools.partial(fused_kernel, zs),
        out_shape=(grad, grad, grad, jax.ShapeDtypeStruct((lines, tokens, width), jnp.float32)),
        in_specs=[vmem] * 10,
        out_specs=[vmem] * 4,
        scratch_shapes=[
            pltpu.VMEM((rows, zs, XS, CORES, tokens, width), big.dtype),
            pltpu.VMEM((zs, XS, CORES) + small.shape, small.dtype),
            block(XS, CORES), block(XS), block(), block(), block(), block(),
            sems(2, zs), sems(2, zs), sems(2, zs), sems(2, zs), sems(2, zs, 2), sems(2, zs, 2), sems(2),
        ] + [sems(zs) for _ in range(6)],
        compiler_params=pltpu.CompilerParams(collective_id=0, has_side_effects=True, vmem_limit_bytes=56 << 20),
        name="fused_grads",
    )(big, small, vq, vk, vv, vg, vl, vd, vw, aw)


def square_sums(tokens):
    values = tokens.astype(jnp.float32)
    return jnp.sum(values * values, axis=(0, 2))


def normalize(tokens, scales, gain_rows):
    return (tokens.astype(jnp.float32) * scales[None, :, None] * gain_rows[:, None, :]).astype(jnp.bfloat16)


def norm_parts(tokens, scales, gain_rows, upstream):
    weighted = upstream * gain_rows[:, None, :]
    unit_rows = tokens.astype(jnp.float32) * scales[None, :, None]
    return (weighted, unit_rows, jnp.sum(weighted * unit_rows, axis=(0, 2)))


def norm_finish(weighted, unit_rows, scales, product, feature_count):
    mean_term = product / feature_count
    return (scales[None, :, None] * (weighted - unit_rows * mean_term[None, :, None])).astype(jnp.bfloat16)


def local(vid_query, vid_key, vid_value, vid_out, vid_grad, vid_lse, vid_mask, aud_query, aud_key, aud_value,
          aud_out, aud_grad, aud_lse, aud_mask, gain_vq, gain_ak, gain_aq, gain_vk):
    heads, video, width = vid_query.shape
    tokens = aud_key.shape[1]
    feature_count = lax.axis_size("head") * heads * width
    zs = lax.axis_size("ctx") // (XS * CORES)
    sums = lax.psum(
        jnp.concatenate([square_sums(a) for a in (vid_query, vid_key, aud_query, aud_key)]), "head")
    scales = lax.rsqrt(sums / feature_count + EPS)
    scale_vq, scale_vk = scales[:video], scales[video:2 * video]
    scale_aq, scale_ak = scales[2 * video:2 * video + tokens], scales[2 * video + tokens:]
    video_delta = jnp.sum(vid_grad.astype(jnp.float32) * vid_out.astype(jnp.float32), axis=2)
    audio_delta = jnp.sum(aud_grad.astype(jnp.float32) * aud_out.astype(jnp.float32), axis=2)
    big = jnp.concatenate(
        [normalize(aud_key, scale_ak, gain_ak), aud_value, normalize(aud_query, scale_aq, gain_aq), aud_grad])
    near = XS * CORES
    lane_owner = jnp.arange(near * tokens) // tokens
    small = jnp.where(
        lane_owner[None] == lax.rem(lax.axis_index("ctx"), near),
        jnp.tile(jnp.concatenate([aud_lse, audio_delta]), (1, near)), 0.0)
    up_vq, up_vk, up_vv, sums = fused(
        zs, big, small, normalize(vid_query, scale_vq, gain_vq), normalize(vid_key, scale_vk, gain_vk), vid_value,
        vid_grad, vid_lse[:, None], video_delta[:, None], vid_mask, aud_mask)
    sums = sums.reshape(3, heads, tokens, width)
    up_ak, up_av, up_aq = sums[0], sums[1], sums[2]
    parts = [
        norm_parts(vid_query, scale_vq, gain_vq, up_vq),
        norm_parts(vid_key, scale_vk, gain_vk, up_vk),
        norm_parts(aud_query, scale_aq, gain_aq, up_aq),
        norm_parts(aud_key, scale_ak, gain_ak, up_ak),
    ]
    product = lax.psum(jnp.concatenate([p[2] for p in parts]), "head")
    cuts = (0, video, 2 * video, 2 * video + tokens, 2 * video + 2 * tokens)
    done = [
        norm_finish(w, u, scales[lo:hi], product[lo:hi], feature_count)
        for (w, u, _), lo, hi in zip(parts, cuts[:-1], cuts[1:])
    ]
    return (done[0], done[1], up_vv.astype(jnp.bfloat16), done[2], done[3], up_av.astype(jnp.bfloat16))


def solution(mesh):
    rows = P("head", "ctx", None)
    line = P("head", "ctx")
    gain = P("head", None)
    return jax.shard_map(
        local,
        mesh=mesh,
        in_specs=(rows, rows, rows, rows, rows, line, rows, rows, rows, rows, rows, rows, line,
                  P("head", None, "ctx"), gain, gain, gain, gain),
        out_specs=(rows,) * 6,
        check_vma=False,
    )
```

```python
import functools

import jax
import jax.numpy as jnp
from jax import lax
from jax.experimental import pallas as pl
from jax.experimental.pallas import tpu as pltpu
from jax.sharding import PartitionSpec as P

EPS = 1e-06
XS = 2
CORES = 2
MESH = pl.DeviceIdType.MESH


def place():
    me = lax.axis_index("ctx")
    return me // (XS * CORES), lax.rem(me // CORES, XS), lax.rem(me, CORES)


def peer(z, x, c):
    return {"ctx": (z * XS + x) * CORES + c}


def enter(z, x, c, zs):
    barrier = pltpu.get_barrier_semaphore()
    targets = [peer(z, x, 1 - c), peer(z, 1 - x, c)]
    targets += [peer(lax.rem(z + d, zs), x, c) for d in range(1, zs)]
    n, h = lax.axis_size("head"), lax.axis_index("head")
    targets += [{"head": lax.rem(h + p, n)} for p in range(1, n)]
    for target in targets:
        pl.semaphore_signal(barrier, inc=1, device_id=target, device_id_type=MESH)
    pl.semaphore_wait(barrier, len(targets))


def rows_dot(left, right):
    return lax.dot_general(left, right, (((1,), (1,)), ((), ())), preferred_element_type=jnp.float32)


def cols_dot(left, right):
    return lax.dot_general(left, right, (((0,), (0,)), ((), ())), preferred_element_type=jnp.float32)


def plain_dot(left, right):
    return lax.dot_general(left, right, (((1,), (0,)), ((), ())), preferred_element_type=jnp.float32)


def tile_terms(keys, values, queries, grads, lse, delta, words, first_key):
    nk, nw = keys.shape[0], words.shape[1]
    scale = keys.shape[1] ** (-0.5)
    key_of = lax.broadcasted_iota(jnp.int32, (nk, nw), 0) + first_key
    word_of = lax.broadcasted_iota(jnp.int32, (nk, nw), 1)
    spread = jnp.where(key_of // 8 == word_of, 1.0, 0.0).astype(jnp.bfloat16)
    spread_words = rows_dot(spread, words).astype(jnp.int32)
    shape = spread_words.shape
    bit = jnp.left_shift(1, lax.rem(lax.broadcasted_iota(jnp.int32, shape, 0), 8))
    keep = jnp.bitwise_and(spread_words, bit) != 0
    probs = jnp.exp(rows_dot(keys, queries) * scale - lse)
    dropped = jnp.where(keep, 2.0 * probs, 0.0).astype(jnp.bfloat16)
    prob_grad = jnp.where(keep, 2.0 * rows_dot(values, grads), 0.0)
    score_grad = (probs * (prob_grad - delta)).astype(jnp.bfloat16)
    return (
        plain_dot(dropped, grads),
        scale * plain_dot(score_grad, queries),
        scale * cols_dot(score_grad, keys),
    )


def fused_kernel(zs, big_ref, small_ref, vq_ref, vk_ref, vv_ref, vg_ref, vl_ref, vd_ref, vw_ref, aw_ref,
                 vid_ref, aud_ref, vgain_ref, again_ref, vscale_ref, ascale_ref,
                 gvq_ref, gvk_ref, gvv_ref, gaq_ref, gak_ref, gav_ref,
                 dvq_ref, dvk_ref, dvv_ref, sum_ref, vprod, vprod_in, aprod, aprod_in, n_send, n_recv,
                 big_out, small_out, part, core_in, x_out, x_in, z_out, z_in,
                 z_send, z_recv, x_send, x_recv, c_send, c_recv, own_sem,
                 pc_send, pc_recv, px_send, px_recv, pz_send, pz_recv):
    z, x, c = place()
    heads = vq_ref.shape[0]
    width = vq_ref.shape[2]
    chunk = XS * CORES * big_ref.shape[1]
    source = [lax.rem(z + zs - d, zs) for d in range(zs)]
    enter(z, x, c, zs)
    pairs = ((big_ref, big_out), (small_ref, small_out))

    def slot(k, zz, xx):
        out = pairs[k][1]
        return out.at[:, zz, xx, c] if k == 0 else out.at[zz, xx, c]

    def copies(here, there, send, recv, target):
        return [pltpu.make_async_remote_copy(
            src_ref=here(k), dst_ref=there(k), send_sem=send(k), recv_sem=recv(k), device_id=target,
            device_id_type=MESH) for k in range(2)]

    own_src = lambda k: pairs[k][0]
    z_copies, x_copies, c_copies = [None], [], [[], []]
    for d in range(zs):
        mine = lambda k, d=d: slot(k, source[d], x)
        other = lambda k, d=d: slot(k, source[d], 1 - x)
        src = mine if d else own_src
        if d:
            z_copies.append(copies(own_src, lambda k: slot(k, z, x), lambda k, d=d: z_send.at[k, d],
                                   lambda k, d=d: z_recv.at[k, d], peer(lax.rem(z + d, zs), x, c)))
        x_copies.append(copies(src, mine, lambda k, d=d: x_send.at[k, d], lambda k, d=d: x_recv.at[k, d],
                               peer(z, 1 - x, c)))
        for side, here, there in ((0, src, mine), (1, other, other)):
            c_copies[side].append(copies(here, there, lambda k, d=d, side=side: c_send.at[k, d, side],
                                         lambda k, d=d, side=side: c_recv.at[k, d, side], peer(z, x, 1 - c)))
    own = [pltpu.make_async_copy(pairs[k][0], slot(k, z, x), own_sem.at[k]) for k in range(2)]
    pc_copies = [pltpu.make_async_remote_copy(
        src_ref=part.at[d, :, :, 1 - c], dst_ref=core_in.at[d], send_sem=pc_send.at[d], recv_sem=pc_recv.at[d],
        device_id=peer(z, x, 1 - c), device_id_type=MESH) for d in range(zs)]
    px_copies = [pltpu.make_async_remote_copy(
        src_ref=x_out.at[d], dst_ref=x_in.at[d], send_sem=px_send.at[d], recv_sem=px_recv.at[d],
        device_id=peer(z, 1 - x, c), device_id_type=MESH) for d in range(zs)]
    pz_copies = [None] + [pltpu.make_async_remote_copy(
        src_ref=z_out.at[d], dst_ref=z_in.at[d], send_sem=pz_send.at[d], recv_sem=pz_recv.at[d],
        device_id=peer(source[d], x, c), device_id_type=MESH) for d in range(1, zs)]

    def start(group):
        for copy in group:
            copy.start()

    def arrive(group):
        for copy in group:
            copy.wait_recv()

    def left(group):
        for copy in group:
            copy.wait_send()

    def compute(d):
        zz = source[d]
        rows = pl.ds(pl.multiple_of(zz * chunk, chunk), chunk)

        def head(h, carry):
            ak, av, aq, ag = (big_out[i * heads + h, zz].reshape(chunk, width) for i in range(4))
            lines = lambda i: sum(
                small_out[zz, xx, cc, pl.ds(i * heads + h, 1), :] for xx in range(XS) for cc in range(CORES))
            value_grad, key_grad, query_grad = tile_terms(
                ak, av, vq_ref[h], vg_ref[h], vl_ref[h], vd_ref[h],
                vw_ref[h].astype(jnp.float32).astype(jnp.bfloat16), zz * chunk)
            aud_words = aw_ref[h, rows, :].astype(jnp.float32).astype(jnp.bfloat16)
            vid_value_grad, vid_key_grad, aud_query_grad = tile_terms(
                vk_ref[h], vv_ref[h], aq, ag, lines(0), lines(1), aud_words, 0)
            for i, total in enumerate((key_grad, value_grad, aud_query_grad)):
                part[d, i * heads + h] = total.astype(part.dtype).reshape(part.shape[2:])
            if d:
                dvq_ref[h] += query_grad
                dvk_ref[h] += vid_key_grad
                dvv_ref[h] += vid_value_grad
            else:
                dvq_ref[h] = query_grad
                dvk_ref[h] = vid_key_grad
                dvv_ref[h] = vid_value_grad
            return carry

        lax.fori_loop(0, heads, head, 0)

    def core_sum(d, side):
        return part[d, :, side, c].astype(jnp.float32) + core_in[d, :, side].astype(jnp.float32)

    def to_x(d):
        pc_copies[d].wait_recv()
        x_out[d] = core_sum(d, 1 - x).astype(x_out.dtype)
        px_copies[d].start()

    def to_z(d):
        px_copies[d].wait_recv()
        both = core_sum(d, x) + x_in[d].astype(jnp.float32)
        if d:
            z_out[d] = both.astype(z_out.dtype)
            pz_copies[d].start()
        else:
            sum_ref[...] = both

    def ready(d):
        arrive(x_copies[d])
        start(c_copies[1][d])
        arrive(c_copies[0][d])
        arrive(c_copies[1][d])

    start(x_copies[0])
    for d in range(1, zs):
        start(z_copies[d])
    start(c_copies[0][0])
    start(own)
    for copy in own:
        copy.wait()
    ready(0)
    compute(0)
    pc_copies[0].start()
    for d in range(1, zs):
        arrive(z_copies[d])
        start(x_copies[d])
        start(c_copies[0][d])
    for d in range(1, zs):
        ready(d)
        compute(d)
        pc_copies[d].start()
        to_x(d)
        if d > 1:
            to_z(d - 1)
    n, me_head = vprod_in.shape[0] + 1, lax.axis_index("head")

    def share(k, mine, theirs):
        group = [pltpu.make_async_remote_copy(
            src_ref=mine, dst_ref=theirs.at[p - 1], send_sem=n_send.at[k, p - 1], recv_sem=n_recv.at[k, p - 1],
            device_id={"head": lax.rem(me_head + p, n)}, device_id_type=MESH) for p in range(1, n)]
        start(group)
        return group

    def product(ups, raws, gains, scale):
        total = sum(ups[h] * gains[h] * (raws[h].astype(jnp.float32) * scale) for h in range(heads))
        return jnp.broadcast_to(jnp.sum(total, axis=1, keepdims=True), total.shape)

    def finish(up, raw, gain, scale, total):
        mean_term = total / (n * heads * width)
        return (scale * (up * gain - raw.astype(jnp.float32) * scale * mean_term)).astype(jnp.bfloat16)

    ups = (dvq_ref, dvk_ref)
    for i in range(2):
        vprod[i] = product(ups[i], vid_ref[i], vgain_ref[i], vscale_ref[i])
    video_share = share(0, vprod, vprod_in)
    for h in range(heads):
        gvv_ref[h] = dvv_ref[h].astype(jnp.bfloat16)
    to_z(zs - 1)
    to_x(0)
    to_z(0)
    for d in range(1, zs):
        pz_copies[d].wait_recv()
        sum_ref[...] += z_in[d].astype(jnp.float32)
    audio_ups = [[sum_ref[(2 - 2 * i) * heads + h] for h in range(heads)] for i in range(2)]
    for i in range(2):
        aprod[i] = product(audio_ups[i], aud_ref[i], again_ref[i], ascale_ref[i])
    audio_share = share(1, aprod, aprod_in)
    arrive(video_share)
    for i, out in enumerate((gvq_ref, gvk_ref)):
        total = vprod[i] + sum(vprod_in[p, i] for p in range(n - 1))
        for h in range(heads):
            out[h] = finish(ups[i][h], vid_ref[i, h], vgain_ref[i, h], vscale_ref[i], total)
    for h in range(heads):
        gav_ref[h] = sum_ref[heads + h].astype(jnp.bfloat16)
    arrive(audio_share)
    for i, out in enumerate((gaq_ref, gak_ref)):
        total = aprod[i] + sum(aprod_in[p, i] for p in range(n - 1))
        for h in range(heads):
            out[h] = finish(audio_ups[i][h], aud_ref[i, h], again_ref[i, h], ascale_ref[i], total)
    left(video_share)
    left(audio_share)
    for d in range(zs):
        if d:
            left(z_copies[d])
        left(x_copies[d])
        left(c_copies[0][d])
        left(c_copies[1][d])
        pc_copies[d].wait_send()
        px_copies[d].wait_send()
        if d:
            pz_copies[d].wait_send()


def fused(zs, big, small, vq, vk, vv, vg, vl, vd, vw, aw, *norms):
    rows, tokens, width = big.shape
    heads = vq.shape[0]
    lines = 3 * heads
    sems = lambda *shape: pltpu.SemaphoreType.DMA(shape)
    block = lambda *lead: pltpu.VMEM((zs, lines) + lead + (tokens, width), jnp.bfloat16)
    video = vq.shape[1]
    n = lax.axis_size("head")
    grad = jax.ShapeDtypeStruct(vq.shape, jnp.bfloat16)
    small_grad = jax.ShapeDtypeStruct((heads, tokens, width), jnp.bfloat16)
    total = lambda *shape: pltpu.VMEM(shape + (width,), jnp.float32)
    vmem = pl.BlockSpec(memory_space=pltpu.VMEM)
    return pl.pallas_call(
        functools.partial(fused_kernel, zs),
        out_shape=(grad,) * 3 + (small_grad,) * 3,
        in_specs=[vmem] * 16,
        out_specs=[vmem] * 6,
        scratch_shapes=[
            total(heads, video), total(heads, video), total(heads, video), total(lines, tokens),
            total(2, video), total(n - 1, 2, video), total(2, tokens), total(n - 1, 2, tokens),
            sems(2, n - 1), sems(2, n - 1),
            pltpu.VMEM((rows, zs, XS, CORES, tokens, width), big.dtype),
            pltpu.VMEM((zs, XS, CORES) + small.shape, small.dtype),
            block(XS, CORES), block(XS), block(), block(), block(), block(),
            sems(2, zs), sems(2, zs), sems(2, zs), sems(2, zs), sems(2, zs, 2), sems(2, zs, 2), sems(2),
        ] + [sems(zs) for _ in range(6)],
        compiler_params=pltpu.CompilerParams(collective_id=0, has_side_effects=True, vmem_limit_bytes=56 << 20),
        name="fused_grads",
    )(big, small, vq, vk, vv, vg, vl, vd, vw, aw, *norms)


def square_sums(tokens):
    values = tokens.astype(jnp.float32)
    return jnp.sum(values * values, axis=(0, 2))


def normalize(tokens, scales, gain_rows):
    return (tokens.astype(jnp.float32) * scales[None, :, None] * gain_rows[:, None, :]).astype(jnp.bfloat16)


def local(vid_query, vid_key, vid_value, vid_out, vid_grad, vid_lse, vid_mask, aud_query, aud_key, aud_value,
          aud_out, aud_grad, aud_lse, aud_mask, gain_vq, gain_ak, gain_aq, gain_vk):
    heads, video, width = vid_query.shape
    tokens = aud_key.shape[1]
    feature_count = lax.axis_size("head") * heads * width
    zs = lax.axis_size("ctx") // (XS * CORES)
    sums = lax.psum(
        jnp.concatenate([square_sums(a) for a in (vid_query, vid_key, aud_query, aud_key)]), "head")
    scales = lax.rsqrt(sums / feature_count + EPS)
    scale_vq, scale_vk = scales[:video], scales[video:2 * video]
    scale_aq, scale_ak = scales[2 * video:2 * video + tokens], scales[2 * video + tokens:]
    video_delta = jnp.sum(vid_grad.astype(jnp.float32) * vid_out.astype(jnp.float32), axis=2)
    audio_delta = jnp.sum(aud_grad.astype(jnp.float32) * aud_out.astype(jnp.float32), axis=2)
    big = jnp.concatenate(
        [normalize(aud_key, scale_ak, gain_ak), aud_value, normalize(aud_query, scale_aq, gain_aq), aud_grad])
    near = XS * CORES
    lane_owner = jnp.arange(near * tokens) // tokens
    small = jnp.where(
        lane_owner[None] == lax.rem(lax.axis_index("ctx"), near),
        jnp.tile(jnp.concatenate([aud_lse, audio_delta]), (1, near)), 0.0)
    return fused(
        zs, big, small, normalize(vid_query, scale_vq, gain_vq), normalize(vid_key, scale_vk, gain_vk), vid_value,
        vid_grad, vid_lse[:, None], video_delta[:, None], vid_mask, aud_mask,
        jnp.stack([vid_query, vid_key]), jnp.stack([aud_query, aud_key]),
        jnp.stack([gain_vq, gain_vk])[:, :, None], jnp.stack([gain_aq, gain_ak])[:, :, None],
        jnp.stack([scale_vq, scale_vk])[..., None], jnp.stack([scale_aq, scale_ak])[..., None])


def solution(mesh):
    rows = P("head", "ctx", None)
    line = P("head", "ctx")
    gain = P("head", None)
    return jax.shard_map(
        local,
        mesh=mesh,
        in_specs=(rows, rows, rows, rows, rows, line, rows, rows, rows, rows, rows, rows, line,
                  P("head", None, "ctx"), gain, gain, gain, gain),
        out_specs=(rows,) * 6,
        check_vma=False,
    )
```
